32 devices in a mesh: axial: 4 (over z), radial: 4 (over y, x), azim: 2 (over core).
Axes of the slice: x: 2, y: 2, z: 4, core: 2. Of those that a mesh axis runs over, the one named last changes fastest.
Arguments:
- source: float32 [3, 64, 64, 256], P(None, 'axial', 'radial', 'azim'), may hold values from -6 to 6
- region: int32 [64, 64, 256], P('axial', 'radial', 'azim'), may hold values from 0 to 401
- fixed_flags: int32 [64, 64, 256], P('axial', 'radial', 'azim'), may hold values 0 or 1
- reluctivity_table: float32 [402], replicated, may hold values from 0.5 to 4
- conductivity_table: float32 [402], replicated, may hold values from 0.5 to 4
Outputs:
- solution: float32 [3, 64, 64, 256], P(None, 'axial', 'radial', 'azim')
- residual: float32 [3, 64, 64, 256], P(None, 'axial', 'radial', 'azim')
The draws below stay inside these ranges and needn't reach their ends.
All inputs are finite; a program needn't handle non-finite values. No bound on the sum of `fixed_flags` on one device may be relied on, other than what follows from the above.
Results may differ from the reference program's by a relative error of at most 0.0003.
Values sent between devices are 32-bit elements; how exact they have to be, the bound alone decides.
A program may use at most 64 MiB of HBM per device.

```python
import math
import jax
import jax.numpy as jnp
from jax import lax

CR = 16
CZ = 128
BA = 8
REGIONS = 402
CYCLES = 2
NS = 2
ES = 2
NA = 64
NR = 64
NZ = 256
N_RADIAL = 4
N_AZIM = 2


def with_ends(values, own_key, least, top_value):
    shape = values.shape
    spot = [jax.random.randint(jax.random.fold_in(own_key, axis), (), 0, shape[axis]) for axis in range(len(shape))]
    values = values.at[tuple(spot)].set(least)
    longest = shape.index(max(shape))
    spot[longest] = (spot[longest] + 1) % shape[longest]
    return values.at[tuple(spot)].set(top_value)


def level_of(own_key, dims, pieces, least, high):
    factor_of = 1.0
    for dim, shards_of in pieces:
        draws = jax.random.uniform(jax.random.fold_in(jax.random.fold_in(own_key, 6), dim), (shards_of,), jnp.float32, least / len(pieces), high / len(pieces))
        factor_of = factor_of * jnp.repeat(jnp.exp(draws), dims[dim] // shards_of).reshape((-1,) + (1,) * (len(dims) - 1 - dim))
    return factor_of


def bell_draw(stream_key, dims, scale, most, shards=(), dtype=jnp.bfloat16):
    factor_of = level_of(stream_key, dims, shards, -0.22, 0.18) if shards else 1.0
    entries = jax.random.normal(stream_key, dims, jnp.float32) * scale * factor_of
    return jnp.minimum(jnp.maximum(entries, -most), most).astype(dtype)


def setup_inputs(seed: int = 0) -> dict:
    splits = jax.random.split(jax.random.key(seed), 6)
    return {
        "source": bell_draw(splits[0], (3, NA, NR, NZ), 1.0, 6.0, ((1, 4), (2, 4), (3, 2)), jnp.float32),
        "region": with_ends(jax.random.randint(splits[1], (NA, NR, NZ), 0, REGIONS), jax.random.fold_in(splits[1], 1), 0, REGIONS - 1).astype(jnp.int32),
        "fixed_flags": with_ends((jax.random.randint(splits[2], (NA, NR, NZ), 0, 8) < 1).astype(jnp.int32), jax.random.fold_in(splits[2], 1), 0, 1),
        "reluctivity_table": jnp.clip(jnp.exp(jax.random.uniform(splits[3], (REGIONS,), jnp.float32, math.log(0.5), math.log(4.0))), 0.5, 4.0),
        "conductivity_table": jnp.clip(jnp.exp(jax.random.uniform(splits[4], (REGIONS,), jnp.float32, math.log(0.5), math.log(4.0))), 0.5, 4.0),
    }


relax_edge = 0.4
relax_node = 0.6
ground_share = 0.01


def unit_step(direction, chosen, elsewhere):
    return tuple(chosen if position == direction else elsewhere for position in range(3))


def window(values, low_cuts, high_cuts):
    extent = values.shape[-3:]
    return values[..., low_cuts[0]:extent[0] - high_cuts[0], low_cuts[1]:extent[1] - high_cuts[1], low_cuts[2]:extent[2] - high_cuts[2]]


def forward_diff(values, direction):
    return window(values, unit_step(direction, 1, 0), unit_step(direction, 0, 1)) - window(values, (0, 0, 0), (1, 1, 1))


def adjoint_diff(values, direction):
    return window(values, unit_step(direction, 0, 1), unit_step(direction, 1, 0)) - window(values, (1, 1, 1), (0, 0, 0))


def apply_operator(padded, reluct_pad, conduct_pad, free_pad):
    face_zero = forward_diff(padded[2], 1) - forward_diff(padded[1], 2)
    face_one = forward_diff(padded[0], 2) - forward_diff(padded[2], 0)
    face_two = forward_diff(padded[1], 0) - forward_diff(padded[0], 1)
    weight = window(reluct_pad, (0, 0, 0), (1, 1, 1))
    field_zero = weight * face_zero
    field_one = weight * face_one
    field_two = weight * face_two
    curl_zero = adjoint_diff(field_one, 2) - adjoint_diff(field_two, 1)
    curl_one = adjoint_diff(field_two, 0) - adjoint_diff(field_zero, 2)
    curl_two = adjoint_diff(field_zero, 1) - adjoint_diff(field_one, 0)
    centred = window(padded, (1, 1, 1), (1, 1, 1))
    result = jnp.stack([curl_zero, curl_one, curl_two]) + window(conduct_pad, (1, 1, 1), (1, 1, 1)) * centred
    return result * window(free_pad, (1, 1, 1), (1, 1, 1))


def edge_region_gradient(padded_nodes):
    return jnp.stack([forward_diff(padded_nodes, direction) for direction in range(3)])


def gradient(padded_nodes):
    return window(edge_region_gradient(padded_nodes), (1, 1, 1), (0, 0, 0))


def grad_adjoint(edges):
    return adjoint_diff(edges[0], 0) + adjoint_diff(edges[1], 1) + adjoint_diff(edges[2], 2)


def lower_shift(values, direction):
    return window(values, unit_step(direction, 0, 1), unit_step(direction, 2, 1))


def inverse_diag(reluct_big, conduct_here, free_here):
    centre = window(reluct_big, (1, 1, 1), (1, 1, 1))
    lower_zero = lower_shift(reluct_big, 0)
    lower_one = lower_shift(reluct_big, 1)
    lower_two = lower_shift(reluct_big, 2)
    diag_zero = 2.0 * centre + lower_one + lower_two + conduct_here
    diag_one = 2.0 * centre + lower_zero + lower_two + conduct_here
    diag_two = 2.0 * centre + lower_zero + lower_one + conduct_here
    diagonal = jnp.stack([diag_zero, diag_one, diag_two])
    return free_here / (diagonal + 1.0 - free_here)


def node_diag(conduct_big):
    centre = window(conduct_big, (1, 1, 1), (1, 1, 1))
    return 3.0 * centre + lower_shift(conduct_big, 0) + lower_shift(conduct_big, 1) + lower_shift(conduct_big, 2)


def global_pad(values, margin):
    leading = [(0, 0)] * (values.ndim - 3)
    wrapped = jnp.pad(values, leading + [(0, 0), (0, 0), (margin, margin)], mode="wrap")
    return jnp.pad(wrapped, leading + [(margin, margin), (margin, margin), (0, 0)])


def reference(source, region, fixed_flags, reluctivity_table, conductivity_table):
    relucts = reluctivity_table[region]
    conduct = conductivity_table[region]
    free_mask = (1 - fixed_flags).astype(jnp.float32)
    reluct_one = global_pad(relucts, 1)
    conduct_one = global_pad(conduct, 1)
    free_one = global_pad(free_mask, 1)
    inverse = inverse_diag(reluct_one, conduct, free_mask)
    node_inverse = 1.0 / node_diag(conduct_one)
    node_weight = window(conduct_one * free_one, (0, 0, 0), (1, 1, 1))
    coarse_count = NA // BA
    blocked = (coarse_count, BA, N_RADIAL, CR, N_AZIM, CZ)
    couplings = jnp.sum(conduct.reshape(blocked)[:, BA - 1], axis=(2, 4))
    grounds = ground_share * jnp.sum(conduct.reshape(blocked)[:, 0], axis=(2, 4))
    lower_coupling = jnp.concatenate([jnp.zeros((1, N_RADIAL, N_AZIM), jnp.float32), couplings[:-1]], axis=0)
    diagonal = lower_coupling + couplings + grounds

    def pivot_step(previous, pair):
        pivot = pair[0] - pair[1] * pair[1] / previous
        return pivot, pivot

    _, pivots = lax.scan(pivot_step, jnp.ones((N_RADIAL, N_AZIM), jnp.float32), (diagonal, lower_coupling))

    def forward_step(previous, trio):
        value = (trio[0] + trio[1] * previous) / trio[2]
        return value, value

    def backward_step(following, trio):
        value = trio[0] + trio[1] / trio[2] * following
        return value, value

    def apply_global(values):
        return apply_operator(global_pad(values, 1), reluct_one, conduct_one, free_one)

    solution = jnp.zeros_like(source)
    residual = free_mask * source
    for cycle_index in range(CYCLES):
        node_res = grad_adjoint(window(global_pad(residual, 1), (0, 0, 0), (1, 1, 1)))
        potential = jnp.zeros_like(node_res)
        for sweep_index in range(NS):
            change = relax_node * node_inverse * node_res
            potential = potential + change
            node_res = node_res - grad_adjoint(node_weight * edge_region_gradient(global_pad(change, 1)))
        totals = jnp.sum(node_res.reshape(blocked), axis=(1, 3, 5))
        _, forward_values = lax.scan(forward_step, jnp.zeros((N_RADIAL, N_AZIM), jnp.float32), (totals, lower_coupling, pivots))
        _, backward_values = lax.scan(backward_step, jnp.zeros((N_RADIAL, N_AZIM), jnp.float32), (forward_values, couplings, pivots), reverse=True)
        spread = backward_values[:, None, :, None, :, None]
        potential = (potential.reshape(blocked) + spread).reshape(NA, NR, NZ)
        correction = gradient(global_pad(potential, 1)) * free_mask
        solution = solution + correction
        residual = residual - apply_global(correction)
        for sweep_index in range(ES):
            change = relax_edge * inverse * residual
            solution = solution + change
            residual = residual - apply_global(change)
    return solution, residual
```

```python
import functools

import jax
import jax.numpy as jnp
from jax import lax
from jax.experimental import pallas as pl
from jax.experimental.pallas import tpu as pltpu
from jax.sharding import PartitionSpec as P

BA = 8
CYCLES = 2
NS = 2
ES = 2
HALO = 4
MESH = pl.DeviceIdType.MESH

relax_edge = 0.4
relax_node = 0.6
ground_share = 0.01

NEIGHBOURS = [(0, -1), (0, 1), (-1, 0), (1, 0), (-1, -1), (-1, 1), (1, -1), (1, 1)]


def kernel(groups, radials, source, region, flags, table, out_sol, out_res,
           pack, swap_in, main, inv, ninv, nres, chg, pot, sol, stage, fin,
           tot_out, tot_in, ysolve, pivs, ends,
           ax0, rs0, rr0, cs0, cr0, ax1, rs1, rr1, cs1, cr1,
           pa0, ps0, pr0, pcs0, pcr0, pa1, ps1, pr1, pcs1, pcr1,
           swap_sems, ex_send, ex_recv, tot_send, tot_recv):
    ax = lax.axis_index("axial")
    rd = lax.axis_index("radial")
    core = lax.axis_index("azim")
    mine = 2 * ax + core
    rows = source.shape[2]
    lanes = source.shape[3]
    frame_rows = main.shape[2]
    wide = main.shape[3]
    first, last = HALO, HALO + BA

    def device(group, radial):
        return {"axial": group // 2, "radial": radial, "azim": lax.rem(group, 2)}

    def when_radial(step):
        if step == 0:
            return lambda f: f()
        ok = rd > 0 if step < 0 else rd < radials - 1
        return pl.when(ok)

    def exists(da, dr):
        ok = None
        if da:
            ok = mine > 0 if da < 0 else mine < groups - 1
        if dr:
            ok_r = rd > 0 if dr < 0 else rd < radials - 1
            ok = ok_r if ok is None else jnp.logical_and(ok, ok_r)
        return ok

    barrier = pltpu.get_barrier_semaphore()

    def each_peer(act):
        for dr in (-1, 0, 1):
            def block(dr=dr):
                for k in range(0 if dr else 1, groups):
                    act(dr, k)
            when_radial(dr)(block)

    def greet(dr, k):
        pl.semaphore_signal(barrier, inc=1, device_id=device(lax.rem(mine + k, groups), rd + dr),
                            device_id_type=MESH)

    each_peer(greet)

    pieces = table.shape[0] // 2
    own_layers = source.shape[1]

    def look(layer, carry):
        free = (1 - flags[layer]).astype(jnp.float32)
        for comp in range(3):
            pack[comp, layer] = free * source[comp, layer]
        for top in range(0, rows, 8):
            ids = region[layer, top:top + 8, :]
            low = jnp.bitwise_and(ids, 127)
            high = lax.shift_right_logical(ids, 7)
            for which in range(2):
                value = jnp.zeros((8, lanes), jnp.float32)
                for piece in range(pieces):
                    row = which * pieces + piece
                    line = jnp.broadcast_to(table[row:row + 1, :], (8, 128))
                    got = jnp.take_along_axis(line, low, axis=1, mode="promise_in_bounds")
                    value = jnp.where(high == piece, got, value)
                pack[3 + which, layer, top:top + 8, :] = value
        pack[5, layer] = free
        return carry

    lax.fori_loop(0, own_layers, look, 0)

    columns = 1 + (rd > 0).astype(jnp.int32) + (rd < radials - 1).astype(jnp.int32)
    pl.semaphore_wait(barrier, columns * groups - 1)

    other = 1 - core
    swap = pltpu.make_async_remote_copy(
        src_ref=pack.at[:, pl.ds(other * BA, BA)], dst_ref=swap_in,
        send_sem=swap_sems.at[0], recv_sem=swap_sems.at[1],
        device_id={"axial": ax, "radial": rd, "azim": other}, device_id_type=MESH)
    swap.start()
    swap.wait()
    is_low = core == 0

    def place(layer, carry):
        for field in range(6):
            here = pack[field, core * BA + layer]
            there = swap_in[field, layer]
            main[field, first + layer, 0:rows, 0:lanes] = jnp.where(is_low, here, there)
            main[field, first + layer, 0:rows, lanes:wide] = jnp.where(is_low, there, here)
        return carry

    lax.fori_loop(0, BA, place, 0)

    sub = lax.broadcasted_iota(jnp.int32, (8, wide), 0)
    low_half = sub < 4

    def turn(value):
        return pltpu.roll(value, 4, axis=0)

    def swap_rows(fields, buf, count, depth, base):
        axial, rsend, rrecv, csend, crecv = buf
        copies = []

        def send(index, da, dr, src, dst):
            copy = pltpu.make_async_remote_copy(
                src_ref=src, dst_ref=dst,
                send_sem=ex_send.at[base + index], recv_sem=ex_recv.at[base + index],
                device_id=device(mine + da, rd + dr), device_id_type=MESH)
            ok = exists(da, dr)
            back = exists(-da, -dr)
            pl.when(ok)(lambda: copy.start())
            copies.append((ok, back, copy))

        send(0, 1, 0, fields.at[0:count, last - depth:last, 0:rows, :], axial.at[0])
        send(1, -1, 0, fields.at[0:count, first:first + depth, 0:rows, :], axial.at[1])

        def pack_rows(dst, layer_lo, half, dr):
            top = rows - 8 if dr > 0 else 0

            def body(pair, carry):
                for field in range(count):
                    a = fields[field, layer_lo + pair, top:top + 8, :]
                    b = fields[field, layer_lo + half + pair, top:top + 8, :]
                    if dr > 0:
                        dst[field, pair] = jnp.where(low_half, turn(b), a)
                    else:
                        dst[field, pair] = jnp.where(low_half, a, turn(b))
                return carry

            lax.fori_loop(0, half, body, 0)

        for index, dr in ((0, 1), (1, -1)):
            pack_rows(rsend.at[index], first, BA // 2, dr)
            send(2 + index, 0, dr, rsend.at[index], rrecv.at[index])
        slot = 0
        for da in (1, -1):
            for dr in (1, -1):
                lo = last - HALO if da > 0 else first
                pack_rows(csend.at[slot], lo, HALO // 2, dr)
                send(4 + slot, da, dr, csend.at[slot], crecv.at[slot])
                slot += 1

        def finish():
            for ok, back, copy in copies:
                pl.when(ok)(lambda copy=copy: copy.wait_send())
                pl.when(back)(lambda copy=copy: copy.wait_recv())
            for index, da in ((0, -1), (1, 1)):
                ok = exists(da, 0)

                def body(layer, carry, index=index, da=da, ok=ok):
                    to = layer + (first - depth if da < 0 else last)
                    for field in range(count):
                        fields[field, to, 0:rows, :] = jnp.where(ok, axial[index, field, layer], 0.0)
                    return carry

                lax.fori_loop(0, depth, body, 0)

            def unpack(from_low, from_up, low_ok, up_ok, layer_lo, half):
                def body(pair, carry):
                    for field in range(count):
                        down = jnp.where(low_ok, from_low[field, pair], 0.0)
                        up = jnp.where(up_ok, from_up[field, pair], 0.0)
                        fields[field, layer_lo + pair, rows:frame_rows, :] = jnp.where(low_half, up, down)
                        fields[field, layer_lo + half + pair, rows:frame_rows, :] = turn(
                            jnp.where(low_half, down, up))
                    return carry

                lax.fori_loop(0, half, body, 0)

            unpack(rrecv.at[0], rrecv.at[1], exists(0, -1), exists(0, 1), first, BA // 2)
            unpack(crecv.at[0], crecv.at[1], exists(-1, -1), exists(-1, 1), first - HALO, HALO // 2)
            unpack(crecv.at[2], crecv.at[3], exists(1, -1), exists(1, 1), last, HALO // 2)

        return finish

    def share(which):
        copies = []

        def build(dr, k):
            peer = lax.rem(mine + k, groups)
            copy = pltpu.make_async_remote_copy(
                src_ref=tot_out.at[which], dst_ref=tot_in.at[which, 1 - dr, mine],
                send_sem=tot_send.at[which, dr + 1, k], recv_sem=tot_recv.at[which, 1 - dr, mine],
                device_id=device(peer, rd + dr), device_id_type=MESH)
            copy.start()

        each_peer(build)
        tot_in[which, 1, mine] = tot_out[which]

        def finish():
            def done(dr, k):
                peer = lax.rem(mine + k, groups)
                copy = pltpu.make_async_remote_copy(
                    src_ref=tot_out.at[which], dst_ref=tot_in.at[which, 1 + dr, peer],
                    send_sem=tot_send.at[which, dr + 1, k], recv_sem=tot_recv.at[which, 1 + dr, peer],
                    device_id=device(peer, rd + dr), device_id_type=MESH)
                copy.wait_send()
                copy.wait_recv()

            each_peer(done)

        return finish

    tile_row = lax.broadcasted_iota(jnp.int32, (8, 128), 0)
    odd = jnp.bitwise_and(tile_row, 1) == 1
    has_low, has_up = exists(0, -1), exists(0, 1)

    def column(which, group, row=0):
        low = jnp.where(has_low, tot_in[which, 0, group, row:row + 8, :], 1.0)
        up = jnp.where(has_up, tot_in[which, 2, group, row:row + 8, :], 1.0)
        here = tot_in[which, 1, group, row:row + 8, :]
        return jnp.where(tile_row < 2, low, jnp.where(tile_row < 4, here, up))

    def halves(value):
        left = jnp.sum(value[:, 0:lanes], keepdims=True)
        right = jnp.sum(value[:, lanes:wide], keepdims=True)
        return jnp.where(odd, jnp.broadcast_to(right, (8, 128)), jnp.broadcast_to(left, (8, 128)))

    bufs_main = (ax0, rs0, rr0, cs0, cr0)
    finish_main = swap_rows(main, bufs_main, 6, 3, 0)
    tot_out[0, 0:8] = halves(main[4, last - 1, 0:rows, :])
    tot_out[0, 8:16] = ground_share * halves(main[4, first, 0:rows, :])
    finish_coef = share(0)
    finish_main()

    def back_r(x):
        return pltpu.roll(x, 1, axis=0)

    def back_l(x):
        return pltpu.roll(x, 1, axis=1)

    def fore_r(x):
        return pltpu.roll(x, frame_rows - 1, axis=0)

    def fore_l(x):
        return pltpu.roll(x, wide - 1, axis=1)

    def setup(layer, carry):
        reluct, conduct, free = main[3, layer], main[4, layer], main[5, layer]
        low0, low1, low2 = main[3, layer - 1], back_r(reluct), back_l(reluct)
        base = 2.0 * reluct + conduct + (1.0 - free)
        scaled = relax_edge * free
        inv[0, layer] = scaled / (base + low1 + low2)
        inv[1, layer] = scaled / (base + low0 + low2)
        inv[2, layer] = scaled / (base + low0 + low1)
        nodes = 3.0 * conduct + main[4, layer - 1] + back_r(conduct) + back_l(conduct)
        inside = conduct > 0.0
        ninv[layer] = jnp.where(inside, relax_node / jnp.where(inside, nodes, 1.0), 0.0)
        return carry

    lax.fori_loop(first - 2, last + 2, setup, 0)

    finish_coef()
    previous = None
    coupling = None
    for group in range(groups):
        nxt = column(0, group)
        ground = column(0, group, 8)
        if group == 0:
            pivot = nxt + ground
            slope = jnp.zeros_like(nxt)
        else:
            pivot = coupling + nxt + ground - coupling * coupling / previous
            slope = coupling
        previous, coupling = pivot, nxt
        pivs[0, group] = 1.0 / pivot
        pivs[1, group] = slope / pivot
        pivs[2, group] = nxt / pivot
    ysolve[0] = jnp.zeros((8, 128), jnp.float32)
    ysolve[groups + 1] = jnp.zeros((8, 128), jnp.float32)

    def sweep(lo, hi, edges, first_cycle):
        def fields_of(layer, u0, u1, u2, up1, up2):
            weight = main[3, layer]
            h1 = weight * (fore_l(u0) - u0 - (up2 - u2))
            h2 = weight * ((up1 - u1) - (fore_r(u0) - u0))
            return weight, h1, h2

        def body(layer, carry):
            u0, u1, u2, h1_low, h2_low = carry
            n0, n1, n2 = edges(layer + 1)
            weight, h1, h2 = fields_of(layer, u0, u1, u2, n1, n2)
            h0 = weight * ((fore_r(u2) - u2) - (fore_l(u1) - u1))
            conduct, free = main[4, layer], main[5, layer]
            a0 = (back_l(h1) - h1) - (back_r(h2) - h2) + conduct * u0
            a1 = (h2_low - h2) - (back_l(h0) - h0) + conduct * u1
            a2 = (back_r(h0) - h0) - (h1_low - h1) + conduct * u2
            main[0, layer] = main[0, layer] - free * a0
            main[1, layer] = main[1, layer] - free * a1
            main[2, layer] = main[2, layer] - free * a2

            @pl.when(jnp.logical_and(layer >= first, layer < last))
            def _():
                for comp, u in enumerate((u0, u1, u2)):
                    if first_cycle:
                        sol[comp, layer - first] = u[0:rows]
                    else:
                        sol[comp, layer - first] = sol[comp, layer - first] + u[0:rows]

            return n0, n1, n2, h1, h2

        b0, b1, b2 = edges(lo - 1)
        c0, c1, c2 = edges(lo)
        _, h1, h2 = fields_of(lo - 1, b0, b1, b2, c1, c2)
        lax.fori_loop(lo, hi, body, (c0, c1, c2, h1, h2))

    def corrections(layer):
        p = pot[0, layer]
        free = main[5, layer]
        return free * (pot[0, layer + 1] - p), free * (fore_r(p) - p), free * (fore_l(p) - p)

    def relaxed(layer):
        return inv[0, layer] * main[0, layer], inv[1, layer] * main[1, layer], inv[2, layer] * main[2, layer]

    def laplace(layer, low_flux):
        p = chg[layer]
        weight = main[4, layer] * main[5, layer]
        f0 = weight * (chg[layer + 1] - p)
        f1 = weight * (fore_r(p) - p)
        f2 = weight * (fore_l(p) - p)
        value = (low_flux - f0) + (back_r(f1) - f1) + (back_l(f2) - f2)
        return value, f0

    def low_flux_of(layer):
        return main[4, layer] * main[5, layer] * (chg[layer + 1] - chg[layer])

    for cycle in range(CYCLES):
        if cycle:
            swap_rows(main, (ax1, rs1, rr1, cs1, cr1), 3, 3, 8)()

        def node(layer, carry):
            r0, r1, r2 = main[0, layer], main[1, layer], main[2, layer]
            value = (main[0, layer - 1] - r0) + (back_r(r1) - r1) + (back_l(r2) - r2)
            nres[layer] = value
            chg[layer] = ninv[layer] * value
            return carry

        lax.fori_loop(first - 2, last + 2, node, 0)

        def second(layer, flux):
            value, flux = laplace(layer, flux)
            value = nres[layer] - value
            nres[layer] = value
            pot[0, layer] = chg[layer]
            return flux

        lax.fori_loop(first - 1, last + 1, second, low_flux_of(first - 2))

        def advance(layer, carry):
            change = ninv[layer] * nres[layer]
            chg[layer] = change
            pot[0, layer] = pot[0, layer] + change
            return carry

        lax.fori_loop(first - 1, last + 1, advance, 0)

        bufs_pot = (pa0, ps0, pr0, pcs0, pcr0) if cycle == 0 else (pa1, ps1, pr1, pcs1, pcr1)
        finish_pot = swap_rows(pot, bufs_pot, 1, 4, 16 + 8 * cycle)

        def total(layer, carry):
            flux, acc = carry
            value, flux = laplace(layer, flux)
            return flux, acc + (nres[layer] - value)[0:rows]

        _, acc = lax.fori_loop(first, last, total,
                               (low_flux_of(first - 1), jnp.zeros((rows, wide), jnp.float32)))
        tot_out[1 + cycle, 0:8] = halves(acc)
        tot_out[1 + cycle, 8:16] = jnp.zeros((8, 128), jnp.float32)
        finish_tot = share(1 + cycle)
        finish_pot()
        finish_tot()

        z = jnp.zeros((8, 128), jnp.float32)
        for group in range(groups):
            z = pivs[0, group] * column(1 + cycle, group) + pivs[1, group] * z
            ysolve[1 + group] = z
        y = jnp.zeros((8, 128), jnp.float32)
        for group in reversed(range(groups)):
            y = ysolve[1 + group] + pivs[2, group] * y
            ysolve[1 + group] = y

        def line(tile, low):
            return jnp.concatenate([tile[low:low + 1, :], tile[low + 1:low + 2, :]], axis=1)

        for part, (lo, hi) in enumerate(((0, first), (first, last), (last, last + HALO))):
            tile = ysolve[mine + part]
            here = jnp.broadcast_to(line(tile, 2), (rows, wide))
            up = jnp.broadcast_to(jnp.where(has_up, line(tile, 4), 0.0), (8, wide))
            down = jnp.broadcast_to(jnp.where(has_low, line(tile, 0), 0.0), (8, wide))
            spread = jnp.concatenate([here, jnp.where(low_half, up, down)], axis=0)

            def lift(layer, carry, spread=spread):
                pot[0, layer] = pot[0, layer] + spread
                return carry

            lax.fori_loop(lo, hi, lift, 0)

        sweep(first - 2, last + 2, corrections, cycle == 0)
        sweep(first - 1, last + 1, relaxed, False)
        sweep(first, last, relaxed, False)

    def split(layer, carry):
        for comp in range(3):
            for which in range(2):
                value = sol[comp, layer] if which == 0 else main[comp, first + layer, 0:rows, :]
                left, right = value[:, 0:lanes], value[:, lanes:wide]
                out = out_sol if which == 0 else out_res
                out[comp, core * BA + layer] = jnp.where(is_low, left, right)
                stage[which, comp, layer] = jnp.where(is_low, right, left)
        return carry

    lax.fori_loop(0, BA, split, 0)
    final = pltpu.make_async_remote_copy(
        src_ref=stage, dst_ref=fin, send_sem=swap_sems.at[2], recv_sem=swap_sems.at[3],
        device_id={"axial": ax, "radial": rd, "azim": other}, device_id_type=MESH)
    final.start()
    final.wait()

    def fetch(layer, carry):
        for comp in range(3):
            out_sol[comp, other * BA + layer] = fin[0, comp, layer]
            out_res[comp, other * BA + layer] = fin[1, comp, layer]
        return carry

    lax.fori_loop(0, BA, fetch, 0)


def on_device(groups, radials, source, region, flags, reluctivity_table, conductivity_table):
    _, layers, rows, lanes = source.shape
    f32 = jnp.float32
    wide = 2 * lanes
    length = reluctivity_table.shape[0]
    pieces = -(-length // 128)
    pad = (0, pieces * 128 - length)
    table = jnp.concatenate([jnp.pad(reluctivity_table, pad).reshape(pieces, 128),
                             jnp.pad(conductivity_table, pad).reshape(pieces, 128)])
    deep, tall = BA + 2 * HALO, rows + 8

    def landing(count, depth):
        return [
            pltpu.VMEM((2, count, depth, rows, wide), f32),
            pltpu.VMEM((2, count, BA // 2, 8, wide), f32),
            pltpu.VMEM((2, count, BA // 2, 8, wide), f32),
            pltpu.VMEM((4, count, HALO // 2, 8, wide), f32),
            pltpu.VMEM((4, count, HALO // 2, 8, wide), f32),
        ]

    vmem = pl.BlockSpec(memory_space=pltpu.VMEM)
    return pl.pallas_call(
        functools.partial(kernel, groups, radials),
        out_shape=(jax.ShapeDtypeStruct(source.shape, f32),) * 2,
        in_specs=[vmem] * 4,
        out_specs=(vmem, vmem),
        scratch_shapes=[
            pltpu.VMEM((6, layers, rows, lanes), f32),
            pltpu.VMEM((6, BA, rows, lanes), f32),
            pltpu.VMEM((6, deep, tall, wide), f32),
            pltpu.VMEM((3, deep, tall, wide), f32),
            pltpu.VMEM((deep, tall, wide), f32),
            pltpu.VMEM((deep, tall, wide), f32),
            pltpu.VMEM((deep, tall, wide), f32),
            pltpu.VMEM((1, deep, tall, wide), f32),
            pltpu.VMEM((3, BA, rows, wide), f32),
            pltpu.VMEM((2, 3, BA, rows, lanes), f32),
            pltpu.VMEM((2, 3, BA, rows, lanes), f32),
            pltpu.VMEM((1 + CYCLES, 16, 128), f32),
            pltpu.VMEM((1 + CYCLES, 3, groups, 16, 128), f32),
            pltpu.VMEM((groups + 2, 8, 128), f32),
            pltpu.VMEM((3, groups, 8, 128), f32),
            pltpu.VMEM((8, 128), f32),
            *landing(6, 3), *landing(3, 3), *landing(1, 4), *landing(1, 4),
            pltpu.SemaphoreType.DMA((4,)),
            pltpu.SemaphoreType.DMA((32,)),
            pltpu.SemaphoreType.DMA((32,)),
            pltpu.SemaphoreType.DMA((1 + CYCLES, 3, groups)),
            pltpu.SemaphoreType.DMA((1 + CYCLES, 3, groups)),
        ],
        compiler_params=pltpu.CompilerParams(
            collective_id=0, has_side_effects=True, vmem_limit_bytes=48 * 1024 * 1024),
    )(source, region, flags, table)


def solution(mesh):
    placed = (
        P(None, "axial", "radial", "azim"),
        P("axial", "radial", "azim"),
        P("axial", "radial", "azim"),
        P(),
        P(),
    )
    out = P(None, "axial", "radial", "azim")
    return jax.shard_map(
        functools.partial(on_device, 2 * mesh.shape["axial"], mesh.shape["radial"]),
        mesh=mesh,
        in_specs=placed,
        out_specs=(out, out),
        check_vma=False,
    )
```

```python
import functools

import jax
import jax.numpy as jnp
from jax import lax
from jax.experimental import pallas as pl
from jax.experimental.pallas import tpu as pltpu
from jax.sharding import PartitionSpec as P

BA = 8
CYCLES = 2
NS = 2
ES = 2
HALO = 4
MESH = pl.DeviceIdType.MESH

relax_edge = 0.4
relax_node = 0.6
ground_share = 0.01

NEIGHBOURS = [(0, -1), (0, 1), (-1, 0), (1, 0), (-1, -1), (-1, 1), (1, -1), (1, 1)]


def kernel(groups, radials, source, region, flags, table, out_sol, out_res,
           pack, swap_in, main, inv, ninv, nres, chg, pot, sol, stage, fin,
           tot_out, tot_in, ysolve, pivs, ends,
           ax0, rs0, rr0, co0, ax1, rs1, rr1, co1,
           pa0, ps0, pr0, pc0, pa1, ps1, pr1, pc1,
           swap_sems, ex_send, ex_recv, tot_send, tot_recv):
    ax = lax.axis_index("axial")
    rd = lax.axis_index("radial")
    core = lax.axis_index("azim")
    mine = 2 * ax + core
    rows = source.shape[2]
    lanes = source.shape[3]
    frame_rows = main.shape[2]
    wide = main.shape[3]
    first, last = HALO, HALO + BA

    def device(group, radial):
        return {"axial": group // 2, "radial": radial, "azim": lax.rem(group, 2)}

    def when_radial(step):
        if step == 0:
            return lambda f: f()
        ok = rd > 0 if step < 0 else rd < radials - 1
        return pl.when(ok)

    def exists(da, dr):
        ok = None
        if da:
            ok = mine > 0 if da < 0 else mine < groups - 1
        if dr:
            ok_r = rd > 0 if dr < 0 else rd < radials - 1
            ok = ok_r if ok is None else jnp.logical_and(ok, ok_r)
        return ok

    barrier = pltpu.get_barrier_semaphore()

    def each_peer(act):
        for dr in (-1, 0, 1):
            def block(dr=dr):
                for k in range(0 if dr else 1, groups):
                    act(dr, k)
            when_radial(dr)(block)

    def greet(dr, k):
        pl.semaphore_signal(barrier, inc=1, device_id=device(lax.rem(mine + k, groups), rd + dr),
                            device_id_type=MESH)

    each_peer(greet)

    pieces = table.shape[0] // 2
    own_layers = source.shape[1]

    def look(layer, carry):
        free = (1 - flags[layer]).astype(jnp.float32)
        for comp in range(3):
            pack[comp, layer] = free * source[comp, layer]
        for top in range(0, rows, 8):
            ids = region[layer, top:top + 8, :]
            low = jnp.bitwise_and(ids, 127)
            high = lax.shift_right_logical(ids, 7)
            for which in range(2):
                value = jnp.zeros((8, lanes), jnp.float32)
                for piece in range(pieces):
                    row = which * pieces + piece
                    line = jnp.broadcast_to(table[row:row + 1, :], (8, 128))
                    got = jnp.take_along_axis(line, low, axis=1, mode="promise_in_bounds")
                    value = jnp.where(high == piece, got, value)
                pack[3 + which, layer, top:top + 8, :] = value
        pack[5, layer] = free
        return carry

    lax.fori_loop(0, own_layers, look, 0)

    columns = 1 + (rd > 0).astype(jnp.int32) + (rd < radials - 1).astype(jnp.int32)
    pl.semaphore_wait(barrier, columns * groups - 1)

    other = 1 - core
    swap = pltpu.make_async_remote_copy(
        src_ref=pack.at[:, pl.ds(other * BA, BA)], dst_ref=swap_in,
        send_sem=swap_sems.at[0], recv_sem=swap_sems.at[1],
        device_id={"axial": ax, "radial": rd, "azim": other}, device_id_type=MESH)
    swap.start()
    swap.wait()
    is_low = core == 0

    def place(layer, carry):
        for field in range(6):
            here = pack[field, core * BA + layer]
            there = swap_in[field, layer]
            main[field, first + layer, 0:rows, 0:lanes] = jnp.where(is_low, here, there)
            main[field, first + layer, 0:rows, lanes:wide] = jnp.where(is_low, there, here)
        return carry

    lax.fori_loop(0, BA, place, 0)

    sub = lax.broadcasted_iota(jnp.int32, (8, wide), 0)
    low_half = sub < 4

    def turn(value):
        return pltpu.roll(value, 4, axis=0)

    pair_of = lax.shift_right_logical(sub, 1)

    def swap_rows(fields, buf, narrow, count, depth, base):
        axial, rsend, rrecv, corner = buf
        tiles = 2 * narrow + (BA // 2) * (count - narrow)
        begun = []

        def send(index, da, dr, src, dst):
            copy = pltpu.make_async_remote_copy(
                src_ref=src, dst_ref=dst,
                send_sem=ex_send.at[base + index], recv_sem=ex_recv.at[base + index],
                device_id=device(mine + da, rd + dr), device_id_type=MESH)
            ok = exists(da, dr)
            pl.when(ok)(lambda: copy.start())
            return (ok, exists(-da, -dr), copy)

        def wait_in(item):
            pl.when(item[1])(lambda: item[2].wait_recv())

        def wait_out(item):
            pl.when(item[0])(lambda: item[2].wait_send())

        for index, dr in ((0, 1), (1, -1)):
            dst = rsend.at[index]
            top = rows - 8 if dr > 0 else 0
            for field in range(narrow):
                for tile in range(2):
                    value = fields[field, first + tile, top:top + 8, :]
                    for step in range(1, 4):
                        more = fields[field, first + tile + 2 * step, top:top + 8, :]
                        spot = 3 - step if dr > 0 else step
                        more = pltpu.roll(more, 8 - 2 * step if dr > 0 else 2 * step, axis=0)
                        value = jnp.where(pair_of == spot, more, value)
                    dst[2 * field + tile] = value
            if narrow and dr > 0:
                value = fields[1, first + 5, top:top + 8, :]
                for layer in range(BA):
                    if layer != 5:
                        more = pltpu.roll(fields[1, first + layer, top:top + 8, :], (layer + 3) % 8, axis=0)
                        value = jnp.where(sub == layer, more, value)
                dst[tiles] = value
            for field in range(narrow, count):
                for pair in range(BA // 2):
                    a = fields[field, first + pair, top:top + 8, :]
                    b = turn(fields[field, first + BA // 2 + pair, top:top + 8, :])
                    at = 2 * narrow + (BA // 2) * (field - narrow) + pair
                    dst[at] = jnp.where(low_half, b, a) if dr > 0 else jnp.where(low_half, a, b)
            size = tiles + 1 if narrow and dr > 0 else tiles
            begun.append(send(2 + index, 0, dr, rsend.at[index, 0:size], rrecv.at[index, 0:size]))

        begun.append(send(0, 1, 0, fields.at[0:count, last - depth:last, 0:rows, :], axial.at[0]))
        begun.append(send(1, -1, 0, fields.at[0:count, first:first + depth, 0:rows, :], axial.at[1]))

        def finish():
            wait_in(begun[0])
            wait_in(begun[1])
            low_ok, up_ok = exists(0, -1), exists(0, 1)
            low, up = rrecv.at[0], rrecv.at[1]
            for field in range(narrow):
                for tile in range(2):
                    down = jnp.where(low_ok, low[2 * field + tile], 0.0)
                    above = jnp.where(up_ok, up[2 * field + tile], 0.0)
                    for step in range(4):
                        layer = tile + 2 * step
                        d = pltpu.roll(down, 2 * step, axis=0) if step else down
                        u = pltpu.roll(above, 8 - 2 * step, axis=0) if step else above
                        value = jnp.where(sub < 2, u, d)
                        if field == 1:
                            extra = jnp.where(low_ok, low[tiles], 0.0)
                            if layer != 5:
                                extra = pltpu.roll(extra, (5 - layer) % 8, axis=0)
                            value = jnp.where(sub == 5, extra, value)
                        fields[field, first + layer, rows:frame_rows, :] = value
            for field in range(narrow, count):
                for pair in range(BA // 2):
                    at = 2 * narrow + (BA // 2) * (field - narrow) + pair
                    down = jnp.where(low_ok, low[at], 0.0)
                    above = jnp.where(up_ok, up[at], 0.0)
                    fields[field, first + pair, rows:frame_rows, :] = jnp.where(low_half, above, down)
                    fields[field, first + BA // 2 + pair, rows:frame_rows, :] = turn(
                        jnp.where(low_half, down, above))
            begun.append(send(4, 1, 0, fields.at[0:count, last - depth:last, rows:frame_rows, :], corner.at[0]))
            begun.append(send(5, -1, 0, fields.at[0:count, first:first + depth, rows:frame_rows, :], corner.at[1]))
            for part, at in ((2, 0), (4, rows)):
                for index, da in ((0, -1), (1, 1)):
                    wait_in(begun[part + index])
                    ok = exists(da, 0)
                    buffer = axial if part == 2 else corner
                    to = first - depth if da < 0 else last

                    def body(layer, carry, index=index, ok=ok, buffer=buffer, to=to, at=at):
                        for field in range(count):
                            fields[field, to + layer, at:(rows if at == 0 else frame_rows), :] = jnp.where(
                                ok, buffer[index, field, layer], 0.0)
                        return carry

                    lax.fori_loop(0, depth, body, 0)
            for item in begun:
                wait_out(item)

        return finish

    def share(which):
        copies = []

        def build(dr, k):
            peer = lax.rem(mine + k, groups)
            copy = pltpu.make_async_remote_copy(
                src_ref=tot_out.at[which], dst_ref=tot_in.at[which, 1 - dr, mine],
                send_sem=tot_send.at[which, dr + 1, k], recv_sem=tot_recv.at[which, 1 - dr, mine],
                device_id=device(peer, rd + dr), device_id_type=MESH)
            copy.start()

        each_peer(build)
        tot_in[which, 1, mine] = tot_out[which]

        def finish():
            def done(dr, k):
                peer = lax.rem(mine + k, groups)
                copy = pltpu.make_async_remote_copy(
                    src_ref=tot_out.at[which], dst_ref=tot_in.at[which, 1 + dr, peer],
                    send_sem=tot_send.at[which, dr + 1, k], recv_sem=tot_recv.at[which, 1 + dr, peer],
                    device_id=device(peer, rd + dr), device_id_type=MESH)
                copy.wait_send()
                copy.wait_recv()

            each_peer(done)

        return finish

    tile_row = lax.broadcasted_iota(jnp.int32, (8, 128), 0)
    odd = jnp.bitwise_and(tile_row, 1) == 1
    has_low, has_up = exists(0, -1), exists(0, 1)

    def column(which, group, row=0):
        low = jnp.where(has_low, tot_in[which, 0, group, row:row + 8, :], 1.0)
        up = jnp.where(has_up, tot_in[which, 2, group, row:row + 8, :], 1.0)
        here = tot_in[which, 1, group, row:row + 8, :]
        return jnp.where(tile_row < 2, low, jnp.where(tile_row < 4, here, up))

    def halves(value):
        left = jnp.sum(value[:, 0:lanes], keepdims=True)
        right = jnp.sum(value[:, lanes:wide], keepdims=True)
        return jnp.where(odd, jnp.broadcast_to(right, (8, 128)), jnp.broadcast_to(left, (8, 128)))

    bufs_main = (ax0, rs0, rr0, co0)
    finish_main = swap_rows(main, bufs_main, 3, 6, 3, 0)
    tot_out[0, 0:8] = halves(main[4, last - 1, 0:rows, :])
    tot_out[0, 8:16] = ground_share * halves(main[4, first, 0:rows, :])
    finish_coef = share(0)
    finish_main()

    def back_r(x):
        return pltpu.roll(x, 1, axis=0)

    def back_l(x):
        return pltpu.roll(x, 1, axis=1)

    def fore_r(x):
        return pltpu.roll(x, frame_rows - 1, axis=0)

    def fore_l(x):
        return pltpu.roll(x, wide - 1, axis=1)

    def setup(layer, carry):
        reluct, conduct, free = main[3, layer], main[4, layer], main[5, layer]
        low0, low1, low2 = main[3, layer - 1], back_r(reluct), back_l(reluct)
        base = 2.0 * reluct + conduct + (1.0 - free)
        scaled = relax_edge * free
        inv[0, layer] = scaled / (base + low1 + low2)
        inv[1, layer] = scaled / (base + low0 + low2)
        inv[2, layer] = scaled / (base + low0 + low1)
        nodes = 3.0 * conduct + main[4, layer - 1] + back_r(conduct) + back_l(conduct)
        inside = conduct > 0.0
        ninv[layer] = jnp.where(inside, relax_node / jnp.where(inside, nodes, 1.0), 0.0)
        return carry

    lax.fori_loop(first - 2, last + 2, setup, 0)

    finish_coef()
    previous = None
    coupling = None
    for group in range(groups):
        nxt = column(0, group)
        ground = column(0, group, 8)
        if group == 0:
            pivot = nxt + ground
            slope = jnp.zeros_like(nxt)
        else:
            pivot = coupling + nxt + ground - coupling * coupling / previous
            slope = coupling
        previous, coupling = pivot, nxt
        pivs[0, group] = 1.0 / pivot
        pivs[1, group] = slope / pivot
        pivs[2, group] = nxt / pivot
    ysolve[0] = jnp.zeros((8, 128), jnp.float32)
    ysolve[groups + 1] = jnp.zeros((8, 128), jnp.float32)

    def sweep(lo, hi, edges, first_cycle):
        def fields_of(layer, u0, u1, u2, up1, up2):
            weight = main[3, layer]
            h1 = weight * (fore_l(u0) - u0 - (up2 - u2))
            h2 = weight * ((up1 - u1) - (fore_r(u0) - u0))
            return weight, h1, h2

        def body(layer, carry):
            u0, u1, u2, h1_low, h2_low = carry
            n0, n1, n2 = edges(layer + 1)
            weight, h1, h2 = fields_of(layer, u0, u1, u2, n1, n2)
            h0 = weight * ((fore_r(u2) - u2) - (fore_l(u1) - u1))
            conduct, free = main[4, layer], main[5, layer]
            a0 = (back_l(h1) - h1) - (back_r(h2) - h2) + conduct * u0
            a1 = (h2_low - h2) - (back_l(h0) - h0) + conduct * u1
            a2 = (back_r(h0) - h0) - (h1_low - h1) + conduct * u2
            main[0, layer] = main[0, layer] - free * a0
            main[1, layer] = main[1, layer] - free * a1
            main[2, layer] = main[2, layer] - free * a2

            @pl.when(jnp.logical_and(layer >= first, layer < last))
            def _():
                for comp, u in enumerate((u0, u1, u2)):
                    if first_cycle:
                        sol[comp, layer - first] = u[0:rows]
                    else:
                        sol[comp, layer - first] = sol[comp, layer - first] + u[0:rows]

            return n0, n1, n2, h1, h2

        b0, b1, b2 = edges(lo - 1)
        c0, c1, c2 = edges(lo)
        _, h1, h2 = fields_of(lo - 1, b0, b1, b2, c1, c2)
        lax.fori_loop(lo, hi, body, (c0, c1, c2, h1, h2))

    def corrections(layer):
        p = pot[0, layer]
        free = main[5, layer]
        return free * (pot[0, layer + 1] - p), free * (fore_r(p) - p), free * (fore_l(p) - p)

    def relaxed(layer):
        return inv[0, layer] * main[0, layer], inv[1, layer] * main[1, layer], inv[2, layer] * main[2, layer]

    def laplace(layer, low_flux):
        p = chg[layer]
        weight = main[4, layer] * main[5, layer]
        f0 = weight * (chg[layer + 1] - p)
        f1 = weight * (fore_r(p) - p)
        f2 = weight * (fore_l(p) - p)
        value = (low_flux - f0) + (back_r(f1) - f1) + (back_l(f2) - f2)
        return value, f0

    def low_flux_of(layer):
        return main[4, layer] * main[5, layer] * (chg[layer + 1] - chg[layer])

    for cycle in range(CYCLES):
        if cycle:
            swap_rows(main, (ax1, rs1, rr1, co1), 3, 3, 3, 8)()

        def node(layer, carry):
            r0, r1, r2 = main[0, layer], main[1, layer], main[2, layer]
            value = (main[0, layer - 1] - r0) + (back_r(r1) - r1) + (back_l(r2) - r2)
            nres[layer] = value
            chg[layer] = ninv[layer] * value
            return carry

        lax.fori_loop(first - 2, last + 2, node, 0)

        def second(layer, flux):
            value, flux = laplace(layer, flux)
            value = nres[layer] - value
            nres[layer] = value
            pot[0, layer] = chg[layer]
            return flux

        lax.fori_loop(first - 1, last + 1, second, low_flux_of(first - 2))

        def advance(layer, carry):
            change = ninv[layer] * nres[layer]
            chg[layer] = change
            pot[0, layer] = pot[0, layer] + change
            return carry

        lax.fori_loop(first - 1, last + 1, advance, 0)

        bufs_pot = (pa0, ps0, pr0, pc0) if cycle == 0 else (pa1, ps1, pr1, pc1)
        finish_pot = swap_rows(pot, bufs_pot, 0, 1, 4, 16 + 8 * cycle)

        def total(layer, carry):
            flux, acc = carry
            value, flux = laplace(layer, flux)
            return flux, acc + (nres[layer] - value)[0:rows]

        _, acc = lax.fori_loop(first, last, total,
                               (low_flux_of(first - 1), jnp.zeros((rows, wide), jnp.float32)))
        tot_out[1 + cycle, 0:8] = halves(acc)
        tot_out[1 + cycle, 8:16] = jnp.zeros((8, 128), jnp.float32)
        finish_tot = share(1 + cycle)
        finish_pot()
        finish_tot()

        z = jnp.zeros((8, 128), jnp.float32)
        for group in range(groups):
            z = pivs[0, group] * column(1 + cycle, group) + pivs[1, group] * z
            ysolve[1 + group] = z
        y = jnp.zeros((8, 128), jnp.float32)
        for group in reversed(range(groups)):
            y = ysolve[1 + group] + pivs[2, group] * y
            ysolve[1 + group] = y

        def line(tile, low):
            return jnp.concatenate([tile[low:low + 1, :], tile[low + 1:low + 2, :]], axis=1)

        for part, (lo, hi) in enumerate(((0, first), (first, last), (last, last + HALO))):
            tile = ysolve[mine + part]
            here = jnp.broadcast_to(line(tile, 2), (rows, wide))
            up = jnp.broadcast_to(jnp.where(has_up, line(tile, 4), 0.0), (8, wide))
            down = jnp.broadcast_to(jnp.where(has_low, line(tile, 0), 0.0), (8, wide))
            spread = jnp.concatenate([here, jnp.where(low_half, up, down)], axis=0)

            def lift(layer, carry, spread=spread):
                pot[0, layer] = pot[0, layer] + spread
                return carry

            lax.fori_loop(lo, hi, lift, 0)

        sweep(first - 2, last + 2, corrections, cycle == 0)
        sweep(first - 1, last + 1, relaxed, False)
        sweep(first, last, relaxed, False)

    def split(layer, carry):
        for comp in range(3):
            for which in range(2):
                value = sol[comp, layer] if which == 0 else main[comp, first + layer, 0:rows, :]
                left, right = value[:, 0:lanes], value[:, lanes:wide]
                out = out_sol if which == 0 else out_res
                out[comp, core * BA + layer] = jnp.where(is_low, left, right)
                stage[which, comp, layer] = jnp.where(is_low, right, left)
        return carry

    lax.fori_loop(0, BA, split, 0)
    final = pltpu.make_async_remote_copy(
        src_ref=stage, dst_ref=fin, send_sem=swap_sems.at[2], recv_sem=swap_sems.at[3],
        device_id={"axial": ax, "radial": rd, "azim": other}, device_id_type=MESH)
    final.start()
    final.wait()

    def fetch(layer, carry):
        for comp in range(3):
            out_sol[comp, other * BA + layer] = fin[0, comp, layer]
            out_res[comp, other * BA + layer] = fin[1, comp, layer]
        return carry

    lax.fori_loop(0, BA, fetch, 0)


def on_device(groups, radials, source, region, flags, reluctivity_table, conductivity_table):
    _, layers, rows, lanes = source.shape
    f32 = jnp.float32
    wide = 2 * lanes
    length = reluctivity_table.shape[0]
    pieces = -(-length // 128)
    pad = (0, pieces * 128 - length)
    table = jnp.concatenate([jnp.pad(reluctivity_table, pad).reshape(pieces, 128),
                             jnp.pad(conductivity_table, pad).reshape(pieces, 128)])
    deep, tall = BA + 2 * HALO, rows + 8

    def landing(narrow, count, depth):
        tiles = 2 * narrow + (BA // 2) * (count - narrow) + (1 if narrow else 0)
        return [
            pltpu.VMEM((2, count, depth, rows, wide), f32),
            pltpu.VMEM((2, tiles, 8, wide), f32),
            pltpu.VMEM((2, tiles, 8, wide), f32),
            pltpu.VMEM((2, count, depth, 8, wide), f32),
        ]

    vmem = pl.BlockSpec(memory_space=pltpu.VMEM)
    return pl.pallas_call(
        functools.partial(kernel, groups, radials),
        out_shape=(jax.ShapeDtypeStruct(source.shape, f32),) * 2,
        in_specs=[vmem] * 4,
        out_specs=(vmem, vmem),
        scratch_shapes=[
            pltpu.VMEM((6, layers, rows, lanes), f32),
            pltpu.VMEM((6, BA, rows, lanes), f32),
            pltpu.VMEM((6, deep, tall, wide), f32),
            pltpu.VMEM((3, deep, tall, wide), f32),
            pltpu.VMEM((deep, tall, wide), f32),
            pltpu.VMEM((deep, tall, wide), f32),
            pltpu.VMEM((deep, tall, wide), f32),
            pltpu.VMEM((1, deep, tall, wide), f32),
            pltpu.VMEM((3, BA, rows, wide), f32),
            pltpu.VMEM((2, 3, BA, rows, lanes), f32),
            pltpu.VMEM((2, 3, BA, rows, lanes), f32),
            pltpu.VMEM((1 + CYCLES, 16, 128), f32),
            pltpu.VMEM((1 + CYCLES, 3, groups, 16, 128), f32),
            pltpu.VMEM((groups + 2, 8, 128), f32),
            pltpu.VMEM((3, groups, 8, 128), f32),
            pltpu.VMEM((8, 128), f32),
            *landing(3, 6, 3), *landing(3, 3, 3), *landing(0, 1, 4), *landing(0, 1, 4),
            pltpu.SemaphoreType.DMA((4,)),
            pltpu.SemaphoreType.DMA((32,)),
            pltpu.SemaphoreType.DMA((32,)),
            pltpu.SemaphoreType.DMA((1 + CYCLES, 3, groups)),
            pltpu.SemaphoreType.DMA((1 + CYCLES, 3, groups)),
        ],
        compiler_params=pltpu.CompilerParams(
            collective_id=0, has_side_effects=True, vmem_limit_bytes=48 * 1024 * 1024),
    )(source, region, flags, table)


def solution(mesh):
    placed = (
        P(None, "axial", "radial", "azim"),
        P("axial", "radial", "azim"),
        P("axial", "radial", "azim"),
        P(),
        P(),
    )
    out = P(None, "axial", "radial", "azim")
    return jax.shard_map(
        functools.partial(on_device, 2 * mesh.shape["axial"], mesh.shape["radial"]),
        mesh=mesh,
        in_specs=placed,
        out_specs=(out, out),
        check_vma=False,
    )
```

```python
import functools

import jax
import jax.numpy as jnp
from jax import lax
from jax.experimental import pallas as pl
from jax.experimental.pallas import tpu as pltpu
from jax.sharding import PartitionSpec as P

BA = 8
CYCLES = 2
NS = 2
ES = 2
HALO = 4
UNROLL = True
MESH = pl.DeviceIdType.MESH

relax_edge = 0.4
relax_node = 0.6
ground_share = 0.01

NEIGHBOURS = [(0, -1), (0, 1), (-1, 0), (1, 0), (-1, -1), (-1, 1), (1, -1), (1, 1)]


def steps(low, high, body, carry):
    return lax.fori_loop(low, high, body, carry, unroll=UNROLL)


def kernel(groups, radials, source, region, flags, table, out_sol, out_res,
           pack, swap_in, main, inv, ninv, nres, chg, pot, sol, stage, fin,
           tot_out, tot_in, ysolve, pivs, ends,
           ax0, rs0, rr0, co0, ax1, rs1, rr1, co1,
           pa0, ps0, pr0, pc0, pa1, ps1, pr1, pc1,
           swap_sems, ex_send, ex_recv, tot_send, tot_recv):
    ax = lax.axis_index("axial")
    rd = lax.axis_index("radial")
    core = lax.axis_index("azim")
    mine = 2 * ax + core
    rows = source.shape[2]
    lanes = source.shape[3]
    frame_rows = main.shape[2]
    wide = main.shape[3]
    first, last = HALO, HALO + BA

    def device(group, radial):
        return {"axial": group // 2, "radial": radial, "azim": lax.rem(group, 2)}

    def when_radial(step):
        if step == 0:
            return lambda f: f()
        ok = rd > 0 if step < 0 else rd < radials - 1
        return pl.when(ok)

    def exists(da, dr):
        ok = None
        if da:
            ok = mine > 0 if da < 0 else mine < groups - 1
        if dr:
            ok_r = rd > 0 if dr < 0 else rd < radials - 1
            ok = ok_r if ok is None else jnp.logical_and(ok, ok_r)
        return ok

    barrier = pltpu.get_barrier_semaphore()

    def each_peer(act):
        for dr in (-1, 0, 1):
            def block(dr=dr):
                for k in range(0 if dr else 1, groups):
                    act(dr, k)
            when_radial(dr)(block)

    def greet(dr, k):
        pl.semaphore_signal(barrier, inc=1, device_id=device(lax.rem(mine + k, groups), rd + dr),
                            device_id_type=MESH)

    each_peer(greet)

    pieces = table.shape[0] // 2
    own_layers = source.shape[1]

    def look(layer, carry):
        free = (1 - flags[layer]).astype(jnp.float32)
        for comp in range(3):
            pack[comp, layer] = free * source[comp, layer]
        for top in range(0, rows, 8):
            ids = region[layer, top:top + 8, :]
            low = jnp.bitwise_and(ids, 127)
            high = lax.shift_right_logical(ids, 7)
            for which in range(2):
                value = jnp.zeros((8, lanes), jnp.float32)
                for piece in range(pieces):
                    row = which * pieces + piece
                    line = jnp.broadcast_to(table[row:row + 1, :], (8, 128))
                    got = jnp.take_along_axis(line, low, axis=1, mode="promise_in_bounds")
                    value = jnp.where(high == piece, got, value)
                pack[3 + which, layer, top:top + 8, :] = value
        pack[5, layer] = free
        return carry

    steps(0, own_layers, look, 0)

    columns = 1 + (rd > 0).astype(jnp.int32) + (rd < radials - 1).astype(jnp.int32)
    pl.semaphore_wait(barrier, columns * groups - 1)

    other = 1 - core
    swap = pltpu.make_async_remote_copy(
        src_ref=pack.at[:, pl.ds(other * BA, BA)], dst_ref=swap_in,
        send_sem=swap_sems.at[0], recv_sem=swap_sems.at[1],
        device_id={"axial": ax, "radial": rd, "azim": other}, device_id_type=MESH)
    swap.start()
    swap.wait()
    is_low = core == 0

    def place(layer, carry):
        for field in range(6):
            here = pack[field, core * BA + layer]
            there = swap_in[field, layer]
            main[field, first + layer, 0:rows, 0:lanes] = jnp.where(is_low, here, there)
            main[field, first + layer, 0:rows, lanes:wide] = jnp.where(is_low, there, here)
        return carry

    steps(0, BA, place, 0)

    sub = lax.broadcasted_iota(jnp.int32, (8, wide), 0)
    low_half = sub < 4

    def turn(value):
        return pltpu.roll(value, 4, axis=0)

    pair_of = lax.shift_right_logical(sub, 1)

    def swap_rows(fields, buf, narrow, count, depth, base):
        axial, rsend, rrecv, corner = buf
        tiles = 2 * narrow + (BA // 2) * (count - narrow)
        begun = []

        def send(index, da, dr, src, dst):
            copy = pltpu.make_async_remote_copy(
                src_ref=src, dst_ref=dst,
                send_sem=ex_send.at[base + index], recv_sem=ex_recv.at[base + index],
                device_id=device(mine + da, rd + dr), device_id_type=MESH)
            ok = exists(da, dr)
            pl.when(ok)(lambda: copy.start())
            return (ok, exists(-da, -dr), copy)

        def wait_in(item):
            pl.when(item[1])(lambda: item[2].wait_recv())

        def wait_out(item):
            pl.when(item[0])(lambda: item[2].wait_send())

        for index, dr in ((0, 1), (1, -1)):
            dst = rsend.at[index]
            top = rows - 8 if dr > 0 else 0
            for field in range(narrow):
                for tile in range(2):
                    value = fields[field, first + tile, top:top + 8, :]
                    for step in range(1, 4):
                        more = fields[field, first + tile + 2 * step, top:top + 8, :]
                        spot = 3 - step if dr > 0 else step
                        more = pltpu.roll(more, 8 - 2 * step if dr > 0 else 2 * step, axis=0)
                        value = jnp.where(pair_of == spot, more, value)
                    dst[2 * field + tile] = value
            if narrow and dr > 0:
                value = fields[1, first + 5, top:top + 8, :]
                for layer in range(BA):
                    if layer != 5:
                        more = pltpu.roll(fields[1, first + layer, top:top + 8, :], (layer + 3) % 8, axis=0)
                        value = jnp.where(sub == layer, more, value)
                dst[tiles] = value
            for field in range(narrow, count):
                for pair in range(BA // 2):
                    a = fields[field, first + pair, top:top + 8, :]
                    b = turn(fields[field, first + BA // 2 + pair, top:top + 8, :])
                    at = 2 * narrow + (BA // 2) * (field - narrow) + pair
                    dst[at] = jnp.where(low_half, b, a) if dr > 0 else jnp.where(low_half, a, b)
            size = tiles + 1 if narrow and dr > 0 else tiles
            begun.append(send(2 + index, 0, dr, rsend.at[index, 0:size], rrecv.at[index, 0:size]))

        begun.append(send(0, 1, 0, fields.at[0:count, last - depth:last, 0:rows, :], axial.at[0]))
        begun.append(send(1, -1, 0, fields.at[0:count, first:first + depth, 0:rows, :], axial.at[1]))

        def finish():
            wait_in(begun[0])
            wait_in(begun[1])
            low_ok, up_ok = exists(0, -1), exists(0, 1)
            low, up = rrecv.at[0], rrecv.at[1]
            for field in range(narrow):
                for tile in range(2):
                    down = jnp.where(low_ok, low[2 * field + tile], 0.0)
                    above = jnp.where(up_ok, up[2 * field + tile], 0.0)
                    for step in range(4):
                        layer = tile + 2 * step
                        d = pltpu.roll(down, 2 * step, axis=0) if step else down
                        u = pltpu.roll(above, 8 - 2 * step, axis=0) if step else above
                        value = jnp.where(sub < 2, u, d)
                        if field == 1:
                            extra = jnp.where(low_ok, low[tiles], 0.0)
                            if layer != 5:
                                extra = pltpu.roll(extra, (5 - layer) % 8, axis=0)
                            value = jnp.where(sub == 5, extra, value)
                        fields[field, first + layer, rows:frame_rows, :] = value
            for field in range(narrow, count):
                for pair in range(BA // 2):
                    at = 2 * narrow + (BA // 2) * (field - narrow) + pair
                    down = jnp.where(low_ok, low[at], 0.0)
                    above = jnp.where(up_ok, up[at], 0.0)
                    fields[field, first + pair, rows:frame_rows, :] = jnp.where(low_half, above, down)
                    fields[field, first + BA // 2 + pair, rows:frame_rows, :] = turn(
                        jnp.where(low_half, down, above))
            begun.append(send(4, 1, 0, fields.at[0:count, last - depth:last, rows:frame_rows, :], corner.at[0]))
            begun.append(send(5, -1, 0, fields.at[0:count, first:first + depth, rows:frame_rows, :], corner.at[1]))
            for part, at in ((2, 0), (4, rows)):
                for index, da in ((0, -1), (1, 1)):
                    wait_in(begun[part + index])
                    ok = exists(da, 0)
                    buffer = axial if part == 2 else corner
                    to = first - depth if da < 0 else last

                    def body(layer, carry, index=index, ok=ok, buffer=buffer, to=to, at=at):
                        for field in range(count):
                            fields[field, to + layer, at:(rows if at == 0 else frame_rows), :] = jnp.where(
                                ok, buffer[index, field, layer], 0.0)
                        return carry

                    steps(0, depth, body, 0)
            for item in begun:
                wait_out(item)

        return finish

    def share(which):
        copies = []

        def build(dr, k):
            peer = lax.rem(mine + k, groups)
            copy = pltpu.make_async_remote_copy(
                src_ref=tot_out.at[which], dst_ref=tot_in.at[which, 1 - dr, mine],
                send_sem=tot_send.at[which, dr + 1, k], recv_sem=tot_recv.at[which, 1 - dr, mine],
                device_id=device(peer, rd + dr), device_id_type=MESH)
            copy.start()

        each_peer(build)
        tot_in[which, 1, mine] = tot_out[which]

        def finish():
            def done(dr, k):
                peer = lax.rem(mine + k, groups)
                copy = pltpu.make_async_remote_copy(
                    src_ref=tot_out.at[which], dst_ref=tot_in.at[which, 1 + dr, peer],
                    send_sem=tot_send.at[which, dr + 1, k], recv_sem=tot_recv.at[which, 1 + dr, peer],
                    device_id=device(peer, rd + dr), device_id_type=MESH)
                copy.wait_send()
                copy.wait_recv()

            each_peer(done)

        return finish

    tile_row = lax.broadcasted_iota(jnp.int32, (8, 128), 0)
    odd = jnp.bitwise_and(tile_row, 1) == 1
    has_low, has_up = exists(0, -1), exists(0, 1)

    def column(which, group, row=0):
        low = jnp.where(has_low, tot_in[which, 0, group, row:row + 8, :], 1.0)
        up = jnp.where(has_up, tot_in[which, 2, group, row:row + 8, :], 1.0)
        here = tot_in[which, 1, group, row:row + 8, :]
        return jnp.where(tile_row < 2, low, jnp.where(tile_row < 4, here, up))

    def halves(value):
        left = jnp.sum(value[:, 0:lanes], keepdims=True)
        right = jnp.sum(value[:, lanes:wide], keepdims=True)
        return jnp.where(odd, jnp.broadcast_to(right, (8, 128)), jnp.broadcast_to(left, (8, 128)))

    bufs_main = (ax0, rs0, rr0, co0)
    finish_main = swap_rows(main, bufs_main, 3, 6, 3, 0)
    tot_out[0, 0:8] = halves(main[4, last - 1, 0:rows, :])
    tot_out[0, 8:16] = ground_share * halves(main[4, first, 0:rows, :])
    finish_coef = share(0)
    finish_main()

    def back_r(x):
        return pltpu.roll(x, 1, axis=0)

    def back_l(x):
        return pltpu.roll(x, 1, axis=1)

    def fore_r(x):
        return pltpu.roll(x, frame_rows - 1, axis=0)

    def fore_l(x):
        return pltpu.roll(x, wide - 1, axis=1)

    def setup(layer, carry):
        reluct, conduct, free = main[3, layer], main[4, layer], main[5, layer]
        low0, low1, low2 = main[3, layer - 1], back_r(reluct), back_l(reluct)
        base = 2.0 * reluct + conduct + (1.0 - free)
        scaled = relax_edge * free
        inv[0, layer] = scaled / (base + low1 + low2)
        inv[1, layer] = scaled / (base + low0 + low2)
        inv[2, layer] = scaled / (base + low0 + low1)
        nodes = 3.0 * conduct + main[4, layer - 1] + back_r(conduct) + back_l(conduct)
        inside = conduct > 0.0
        ninv[layer] = jnp.where(inside, relax_node / jnp.where(inside, nodes, 1.0), 0.0)
        return carry

    steps(first - 2, last + 2, setup, 0)

    finish_coef()
    previous = None
    coupling = None
    for group in range(groups):
        nxt = column(0, group)
        ground = column(0, group, 8)
        if group == 0:
            pivot = nxt + ground
            slope = jnp.zeros_like(nxt)
        else:
            pivot = coupling + nxt + ground - coupling * coupling / previous
            slope = coupling
        previous, coupling = pivot, nxt
        pivs[0, group] = 1.0 / pivot
        pivs[1, group] = slope / pivot
        pivs[2, group] = nxt / pivot
    ysolve[0] = jnp.zeros((8, 128), jnp.float32)
    ysolve[groups + 1] = jnp.zeros((8, 128), jnp.float32)

    def sweep(lo, hi, edges, first_cycle):
        def fields_of(layer, u0, u1, u2, up1, up2):
            weight = main[3, layer]
            h1 = weight * (fore_l(u0) - u0 - (up2 - u2))
            h2 = weight * ((up1 - u1) - (fore_r(u0) - u0))
            return weight, h1, h2

        def body(layer, carry):
            u0, u1, u2, h1_low, h2_low = carry
            n0, n1, n2 = edges(layer + 1)
            weight, h1, h2 = fields_of(layer, u0, u1, u2, n1, n2)
            h0 = weight * ((fore_r(u2) - u2) - (fore_l(u1) - u1))
            conduct, free = main[4, layer], main[5, layer]
            a0 = (back_l(h1) - h1) - (back_r(h2) - h2) + conduct * u0
            a1 = (h2_low - h2) - (back_l(h0) - h0) + conduct * u1
            a2 = (back_r(h0) - h0) - (h1_low - h1) + conduct * u2
            main[0, layer] = main[0, layer] - free * a0
            main[1, layer] = main[1, layer] - free * a1
            main[2, layer] = main[2, layer] - free * a2

            @pl.when(jnp.logical_and(layer >= first, layer < last))
            def _():
                for comp, u in enumerate((u0, u1, u2)):
                    if first_cycle:
                        sol[comp, layer - first] = u[0:rows]
                    else:
                        sol[comp, layer - first] = sol[comp, layer - first] + u[0:rows]

            return n0, n1, n2, h1, h2

        b0, b1, b2 = edges(lo - 1)
        c0, c1, c2 = edges(lo)
        _, h1, h2 = fields_of(lo - 1, b0, b1, b2, c1, c2)
        steps(lo, hi, body, (c0, c1, c2, h1, h2))

    def corrections(layer):
        p = pot[0, layer]
        free = main[5, layer]
        return free * (pot[0, layer + 1] - p), free * (fore_r(p) - p), free * (fore_l(p) - p)

    def relaxed(layer):
        return inv[0, layer] * main[0, layer], inv[1, layer] * main[1, layer], inv[2, layer] * main[2, layer]

    def laplace(layer, low_flux):
        p = chg[layer]
        weight = main[4, layer] * main[5, layer]
        f0 = weight * (chg[layer + 1] - p)
        f1 = weight * (fore_r(p) - p)
        f2 = weight * (fore_l(p) - p)
        value = (low_flux - f0) + (back_r(f1) - f1) + (back_l(f2) - f2)
        return value, f0

    def low_flux_of(layer):
        return main[4, layer] * main[5, layer] * (chg[layer + 1] - chg[layer])

    for cycle in range(CYCLES):
        if cycle:
            swap_rows(main, (ax1, rs1, rr1, co1), 3, 3, 3, 8)()

        def node(layer, carry):
            r0, r1, r2 = main[0, layer], main[1, layer], main[2, layer]
            value = (main[0, layer - 1] - r0) + (back_r(r1) - r1) + (back_l(r2) - r2)
            nres[layer] = value
            chg[layer] = ninv[layer] * value
            return carry

        steps(first - 2, last + 2, node, 0)

        def second(layer, flux):
            value, flux = laplace(layer, flux)
            value = nres[layer] - value
            nres[layer] = value
            pot[0, layer] = chg[layer]
            return flux

        steps(first - 1, last + 1, second, low_flux_of(first - 2))

        def advance(layer, carry):
            change = ninv[layer] * nres[layer]
            chg[layer] = change
            pot[0, layer] = pot[0, layer] + change
            return carry

        steps(first - 1, last + 1, advance, 0)

        bufs_pot = (pa0, ps0, pr0, pc0) if cycle == 0 else (pa1, ps1, pr1, pc1)
        finish_pot = swap_rows(pot, bufs_pot, 0, 1, 4, 16 + 8 * cycle)

        def total(layer, carry):
            flux, acc = carry
            value, flux = laplace(layer, flux)
            return flux, acc + (nres[layer] - value)[0:rows]

        _, acc = steps(first, last, total,
                               (low_flux_of(first - 1), jnp.zeros((rows, wide), jnp.float32)))
        tot_out[1 + cycle, 0:8] = halves(acc)
        tot_out[1 + cycle, 8:16] = jnp.zeros((8, 128), jnp.float32)
        finish_tot = share(1 + cycle)
        finish_pot()
        finish_tot()

        z = jnp.zeros((8, 128), jnp.float32)
        for group in range(groups):
            z = pivs[0, group] * column(1 + cycle, group) + pivs[1, group] * z
            ysolve[1 + group] = z
        y = jnp.zeros((8, 128), jnp.float32)
        for group in reversed(range(groups)):
            y = ysolve[1 + group] + pivs[2, group] * y
            ysolve[1 + group] = y

        def line(tile, low):
            return jnp.concatenate([tile[low:low + 1, :], tile[low + 1:low + 2, :]], axis=1)

        for part, (lo, hi) in enumerate(((0, first), (first, last), (last, last + HALO))):
            tile = ysolve[mine + part]
            here = jnp.broadcast_to(line(tile, 2), (rows, wide))
            up = jnp.broadcast_to(jnp.where(has_up, line(tile, 4), 0.0), (8, wide))
            down = jnp.broadcast_to(jnp.where(has_low, line(tile, 0), 0.0), (8, wide))
            spread = jnp.concatenate([here, jnp.where(low_half, up, down)], axis=0)

            def lift(layer, carry, spread=spread):
                pot[0, layer] = pot[0, layer] + spread
                return carry

            steps(lo, hi, lift, 0)

        sweep(first - 2, last + 2, corrections, cycle == 0)
        sweep(first - 1, last + 1, relaxed, False)
        sweep(first, last, relaxed, False)

    def split(layer, carry):
        for comp in range(3):
            for which in range(2):
                value = sol[comp, layer] if which == 0 else main[comp, first + layer, 0:rows, :]
                left, right = value[:, 0:lanes], value[:, lanes:wide]
                out = out_sol if which == 0 else out_res
                out[comp, core * BA + layer] = jnp.where(is_low, left, right)
                stage[which, comp, layer] = jnp.where(is_low, right, left)
        return carry

    steps(0, BA, split, 0)
    final = pltpu.make_async_remote_copy(
        src_ref=stage, dst_ref=fin, send_sem=swap_sems.at[2], recv_sem=swap_sems.at[3],
        device_id={"axial": ax, "radial": rd, "azim": other}, device_id_type=MESH)
    final.start()
    final.wait()

    def fetch(layer, carry):
        for comp in range(3):
            out_sol[comp, other * BA + layer] = fin[0, comp, layer]
            out_res[comp, other * BA + layer] = fin[1, comp, layer]
        return carry

    steps(0, BA, fetch, 0)


def on_device(groups, radials, source, region, flags, reluctivity_table, conductivity_table):
    _, layers, rows, lanes = source.shape
    f32 = jnp.float32
    wide = 2 * lanes
    length = reluctivity_table.shape[0]
    pieces = -(-length // 128)
    pad = (0, pieces * 128 - length)
    table = jnp.concatenate([jnp.pad(reluctivity_table, pad).reshape(pieces, 128),
                             jnp.pad(conductivity_table, pad).reshape(pieces, 128)])
    deep, tall = BA + 2 * HALO, rows + 8

    def landing(narrow, count, depth):
        tiles = 2 * narrow + (BA // 2) * (count - narrow) + (1 if narrow else 0)
        return [
            pltpu.VMEM((2, count, depth, rows, wide), f32),
            pltpu.VMEM((2, tiles, 8, wide), f32),
            pltpu.VMEM((2, tiles, 8, wide), f32),
            pltpu.VMEM((2, count, depth, 8, wide), f32),
        ]

    vmem = pl.BlockSpec(memory_space=pltpu.VMEM)
    return pl.pallas_call(
        functools.partial(kernel, groups, radials),
        out_shape=(jax.ShapeDtypeStruct(source.shape, f32),) * 2,
        in_specs=[vmem] * 4,
        out_specs=(vmem, vmem),
        scratch_shapes=[
            pltpu.VMEM((6, layers, rows, lanes), f32),
            pltpu.VMEM((6, BA, rows, lanes), f32),
            pltpu.VMEM((6, deep, tall, wide), f32),
            pltpu.VMEM((3, deep, tall, wide), f32),
            pltpu.VMEM((deep, tall, wide), f32),
            pltpu.VMEM((deep, tall, wide), f32),
            pltpu.VMEM((deep, tall, wide), f32),
            pltpu.VMEM((1, deep, tall, wide), f32),
            pltpu.VMEM((3, BA, rows, wide), f32),
            pltpu.VMEM((2, 3, BA, rows, lanes), f32),
            pltpu.VMEM((2, 3, BA, rows, lanes), f32),
            pltpu.VMEM((1 + CYCLES, 16, 128), f32),
            pltpu.VMEM((1 + CYCLES, 3, groups, 16, 128), f32),
            pltpu.VMEM((groups + 2, 8, 128), f32),
            pltpu.VMEM((3, groups, 8, 128), f32),
            pltpu.VMEM((8, 128), f32),
            *landing(3, 6, 3), *landing(3, 3, 3), *landing(0, 1, 4), *landing(0, 1, 4),
            pltpu.SemaphoreType.DMA((4,)),
            pltpu.SemaphoreType.DMA((32,)),
            pltpu.SemaphoreType.DMA((32,)),
            pltpu.SemaphoreType.DMA((1 + CYCLES, 3, groups)),
            pltpu.SemaphoreType.DMA((1 + CYCLES, 3, groups)),
        ],
        compiler_params=pltpu.CompilerParams(
            collective_id=0, has_side_effects=True, vmem_limit_bytes=48 * 1024 * 1024),
    )(source, region, flags, table)


def solution(mesh):
    placed = (
        P(None, "axial", "radial", "azim"),
        P("axial", "radial", "azim"),
        P("axial", "radial", "azim"),
        P(),
        P(),
    )
    out = P(None, "axial", "radial", "azim")
    return jax.shard_map(
        functools.partial(on_device, 2 * mesh.shape["axial"], mesh.shape["radial"]),
        mesh=mesh,
        in_specs=placed,
        out_specs=(out, out),
        check_vma=False,
    )
```
